32 devices in a mesh: inst: 2 (over x), cell: 16 (over z, y, core).
Axes of the slice: x: 2, y: 2, z: 4, core: 2. Of those that a mesh axis runs over, the one named last changes fastest.
Arguments:
- adjoint: float32 [16, 6, 16384], P('inst', None, 'cell'), may hold values from -6 to 6
- source: float32 [16, 6, 16384], P('inst', None, 'cell'), may hold values from -6 to 6
- jac_diag: bfloat16 [16, 6, 6, 16384], P('inst', None, None, 'cell'), may hold values from -6 to 6
- jac_face: bfloat16 [16, 4, 6, 6, 16384], P('inst', None, None, None, 'cell'), may hold values from -4 to 4
- tile_nbr: int32 [128, 4], P('cell'), may hold values from 0 to 7
- dtau: float32 [16384], P('cell'), may hold values from 0.1 to 0.5
- fringe_src: int32 [16, 16, 64], P('cell'), may hold values from 0 to 1023
- fringe_wt: float32 [16, 16, 64], P('cell'), may hold values from 0.2 to 1
- fringe_count: int32 [16, 16], P('cell'), may hold values from 0 to 64, as said below
- fringe_dst: int32 [16, 16, 64], P(None, 'cell'), may hold values from 0 to 1023
Outputs:
- updated: float32 [16, 6, 16384], P('inst', None, 'cell')
The draws below stay inside these ranges and needn't reach their ends.
Inputs may be any that keep to these rules, and one draw needn't show every extreme that they name: `fringe_count`: each group sends 64 live slots to at least one donor owner; group loads differ by up to four times.
All inputs are finite; a program needn't handle non-finite values.
Results may differ from the reference program's by a relative error of at most 0.0003.
Values sent between devices are 32-bit elements; how exact they have to be, the bound alone decides.
A program may use at most 64 MiB of HBM per device.

```python
import math
import jax
import jax.numpy as jnp
from jax import lax

INSTANCES = 16
VARS = 6
FACES = 4
TILE = 128
CELLS_DEV = 1024
CAP = 64
TILES_DEV = 8
CELLS = 16384
TILES = 128
PEERS = 16


def draw_fringe_count(key, part):
    key_base = jax.random.fold_in(key, 11)
    key_heavy = jax.random.fold_in(key, 12)
    key_pick = jax.random.fold_in(key, 13)
    base = jax.random.randint(key_base, (PEERS, PEERS), 0, CAP + 1)
    heavy = jax.random.randint(key_heavy, (PEERS, 1), 1, 5)
    counts = jnp.minimum(base * heavy // 4, CAP)
    pick = jax.random.randint(key_pick, (PEERS, 1), 0, PEERS)
    column = jnp.arange(PEERS, dtype=jnp.int32)[None, :]
    return jnp.where(column == pick, CAP, counts).astype(jnp.int32)


def touch_ends(array, rng, low, high):
    longest = array.shape.index(max(array.shape))
    spots = []
    for shift in (0, 1):
        where = [jax.random.randint(jax.random.fold_in(rng, axis), (), 0, length) for axis, length in enumerate(array.shape)]
        where[longest] = (where[longest] + shift) % array.shape[longest]
        spots.append(tuple(where))
    return array.at[spots[0]].set(low).at[spots[1]].set(high)


def block_levels(own_key, dims, split, low, high):
    def one(axis_at, parts):
        draws = jax.random.uniform(jax.random.fold_in(jax.random.fold_in(own_key, 6), axis_at), (parts,), jnp.float32, low / len(split), high / len(split))
        return jnp.repeat(jnp.exp(draws), dims[axis_at] // parts).reshape((-1,) + (1,) * (len(dims) - axis_at - 1))

    factor_of = one(*split[0])
    for cut in split[1:]:
        factor_of = factor_of * one(*cut)
    return factor_of


def gaussian(rng, extent, scale, bound, pieces=(), kind=jnp.bfloat16):
    array = jax.random.normal(rng, extent, jnp.float32) * scale
    if len(pieces) > 0:
        array = block_levels(rng, extent, pieces, -0.22, 0.18) * array
    return jnp.clip(array, min=-bound, max=bound).astype(kind)


def setup_inputs(seed: int = 0) -> dict:
    streams_of = jax.random.split(jax.random.key(seed), 11)
    return {
        "adjoint": gaussian(streams_of[0], (INSTANCES, VARS, CELLS), 1.0, 6.0, ((0, 2), (2, 16)), jnp.float32),
        "source": gaussian(streams_of[1], (INSTANCES, VARS, CELLS), 1.0, 6.0, ((0, 2), (2, 16)), jnp.float32),
        "jac_diag": gaussian(streams_of[2], (INSTANCES, VARS, VARS, CELLS), 0.4, 6.0, ((0, 2), (3, 16))),
        "jac_face": gaussian(streams_of[3], (INSTANCES, FACES, VARS, VARS, CELLS), 0.25, 4.0, ((0, 2), (4, 16))),
        "tile_nbr": touch_ends(jax.random.randint(streams_of[4], (TILES, FACES), 0, TILES_DEV), jax.random.fold_in(streams_of[4], 1), 0, TILES_DEV - 1).astype(jnp.int32),
        "dtau": jnp.clip(jnp.exp(math.log(0.5) - 1.609438 * jax.random.uniform(streams_of[5], (CELLS,), jnp.float32) ** block_levels(streams_of[5], (CELLS,), ((0, 16),), -0.2, 0.2)), 0.1, 0.5),
        "fringe_src": touch_ends(jax.random.randint(streams_of[6], (PEERS, PEERS, CAP), 0, CELLS_DEV), jax.random.fold_in(streams_of[6], 1), 0, CELLS_DEV - 1).astype(jnp.int32),
        "fringe_wt": jnp.clip(0.2 + 0.8 * jax.random.uniform(streams_of[7], (PEERS, PEERS, CAP), jnp.float32) ** block_levels(streams_of[7], (PEERS, PEERS, CAP), ((0, 16),), -0.2, 0.2), 0.2, 1.0),
        "fringe_count": draw_fringe_count(jax.random.fold_in(streams_of[10], 71), 0),
        "fringe_dst": touch_ends(jax.random.randint(streams_of[9], (PEERS, PEERS, CAP), 0, CELLS_DEV), jax.random.fold_in(streams_of[9], 1), 0, CELLS_DEV - 1).astype(jnp.int32),
    }


def spectral_matrix(count):
    rows = jnp.arange(count, dtype=jnp.int32)[:, None]
    cols = jnp.arange(count, dtype=jnp.int32)[None, :]
    offset = rows - cols
    angle = offset.astype(jnp.float32) * (jnp.pi / count)
    parity = jnp.where(offset % 2 == 0, 1.0, -1.0).astype(jnp.float32)
    denom = jnp.where(offset == 0, 1.0, jnp.sin(angle))
    value = 0.25 * parity * jnp.cos(angle) / denom
    return jnp.where(offset == 0, 0.0, value).astype(jnp.float32)


def reference(adjoint, source, jac_diag, jac_face, tile_nbr, dtau, fringe_src, fringe_wt, fringe_count, fringe_dst):
    smat = spectral_matrix(INSTANCES)
    temporal = jnp.einsum("ji,jac->iac", smat, adjoint, precision=lax.Precision.HIGHEST)
    own = jnp.sum(jac_diag.astype(jnp.float32) * adjoint[:, :, None, :], axis=1)
    tiles = adjoint.reshape(INSTANCES, VARS, TILES, TILE)
    group = (jnp.arange(TILES, dtype=jnp.int32) // TILES_DEV) * TILES_DEV
    faced = jnp.zeros_like(adjoint)
    for face in range(FACES):
        neighbour = (group + tile_nbr[:, face]).astype(jnp.int32)
        near = tiles[:, :, neighbour, :].reshape(INSTANCES, VARS, CELLS)
        faced = faced + jnp.sum(jac_face[:, face].astype(jnp.float32) * near[:, :, None, :], axis=1)
    peers = jnp.arange(PEERS, dtype=jnp.int32)
    src_global = (peers[:, None, None] * CELLS_DEV + fringe_src).reshape(-1)
    dst_global = (peers[None, :, None] * CELLS_DEV + fringe_dst).reshape(-1)
    live = jnp.arange(CAP, dtype=jnp.int32)[None, None, :] < fringe_count[:, :, None]
    coef = jnp.where(live, fringe_wt, 0.0).reshape(-1)
    values = adjoint[:, :, src_global] * coef
    fringe = jnp.zeros_like(adjoint).at[:, :, dst_global].add(values)
    total = own + faced + temporal + fringe - source
    return adjoint - dtau[None, None, :] * total
```

```python
import functools
import math

import jax
import jax.numpy as jnp
import ml_dtypes
import numpy as np
from jax import lax
from jax.experimental import pallas as pl
from jax.experimental.pallas import tpu as pltpu
from jax.sharding import PartitionSpec as P

INSTANCES = 16
FACES = 4
TILE = 128
VARS = 6
MESH = pl.DeviceIdType.MESH


def spectral_matrix(count):
    rows = jnp.arange(count, dtype=jnp.int32)[:, None]
    cols = jnp.arange(count, dtype=jnp.int32)[None, :]
    offset = rows - cols
    angle = offset.astype(jnp.float32) * (jnp.pi / count)
    parity = jnp.where(offset % 2 == 0, 1.0, -1.0).astype(jnp.float32)
    denom = jnp.where(offset == 0, 1.0, jnp.sin(angle))
    value = 0.25 * parity * jnp.cos(angle) / denom
    return jnp.where(offset == 0, 0.0, value)


def pick_rows(flat, sources, weights, block):
    cells_dev = flat.shape[1]
    nblocks = sources.shape[0] // block
    cell_ids = jnp.arange(cells_dev, dtype=jnp.int32)[:, None]

    def one_block(pair):
        index_block, weight_block = pair
        select = jnp.where(cell_ids == index_block[None, :], weight_block[None, :], 0.0)
        return jnp.dot(
            flat, select, precision=lax.Precision.HIGHEST, preferred_element_type=jnp.float32
        )

    result = lax.map(one_block, (sources.reshape(nblocks, block), weights.reshape(nblocks, block)))
    return jnp.transpose(result, (1, 0, 2)).reshape(flat.shape[0], -1)


def place_rows(values, targets, cells_dev, block):
    nblocks = targets.shape[0] // block
    cell_ids = jnp.arange(cells_dev, dtype=jnp.int32)[None, :]

    def add_block(step, total):
        start = step * block
        target_block = lax.dynamic_slice_in_dim(targets, start, block, 0)
        value_block = lax.dynamic_slice_in_dim(values, start, block, 1)
        select = jnp.where(target_block[:, None] == cell_ids, 1.0, 0.0).astype(jnp.float32)
        return total + jnp.dot(
            value_block, select, precision=lax.Precision.HIGHEST, preferred_element_type=jnp.float32
        )

    empty = jnp.zeros((values.shape[0], cells_dev), jnp.float32)
    return lax.fori_loop(0, nblocks, add_block, empty)


def on_device(
    adjoint,
    source,
    jac_diag,
    jac_face,
    tile_nbr,
    dtau,
    fringe_src,
    fringe_wt,
    fringe_count,
    fringe_dst,
):
    inst_dev, nvars, cells_dev = adjoint.shape
    tiles_dev = cells_dev // TILE
    peer_count, slot_cap = (fringe_wt.shape[1], fringe_wt.shape[2])
    total_slots = peer_count * slot_cap
    block = math.gcd(total_slots, 512)
    smat = spectral_matrix(INSTANCES)
    flat = adjoint.reshape(inst_dev * nvars, cells_dev)
    live = jnp.arange(slot_cap, dtype=jnp.int32)[None, :] < fringe_count[0][:, None]
    coef = jnp.where(live, fringe_wt[0], 0.0).reshape(-1)
    picked = pick_rows(flat, fringe_src[0].reshape(-1), coef, block)
    outgoing = picked.reshape(inst_dev, nvars, peer_count, slot_cap)
    arrived = lax.all_to_all(outgoing, "cell", split_axis=2, concat_axis=2, tiled=True)
    spread = lax.all_to_all(adjoint, "inst", split_axis=2, concat_axis=0, tiled=True)
    mixed = jnp.einsum("ji,jac->iac", smat, spread, precision=lax.Precision.HIGHEST)
    temporal = lax.all_to_all(mixed, "inst", split_axis=0, concat_axis=2, tiled=True)
    own = jnp.sum(jac_diag.astype(jnp.float32) * adjoint[:, :, None, :], axis=1)
    tiles = adjoint.reshape(inst_dev, nvars, tiles_dev, TILE)
    tile_ids = jnp.arange(tiles_dev, dtype=jnp.int32)[None, :]
    faced = jnp.zeros_like(adjoint)
    for face in range(FACES):
        select = jnp.where(tile_nbr[:, face][:, None] == tile_ids, 1.0, 0.0).astype(jnp.float32)
        near = jnp.einsum("tu,iaup->iatp", select, tiles, precision=lax.Precision.HIGHEST)
        near = near.reshape(inst_dev, nvars, cells_dev)
        faced = faced + jnp.sum(jac_face[:, face].astype(jnp.float32) * near[:, :, None, :], axis=1)
    donors = fringe_dst[:, 0, :].reshape(-1)
    fringe = place_rows(arrived.reshape(inst_dev * nvars, -1), donors, cells_dev, block)
    fringe = fringe.reshape(inst_dev, nvars, cells_dev)
    total = own + faced + temporal + fringe - source
    return adjoint - dtau[None, None, :] * total


def spectral_blocks(inst_count, inst_dev):
    offset = np.arange(INSTANCES)[:, None] - np.arange(INSTANCES)[None, :]
    angle = offset * (np.pi / INSTANCES)
    parity = np.where(offset % 2 == 0, 1.0, -1.0)
    denom = np.where(offset == 0, 1.0, np.sin(angle))
    smat = np.where(offset == 0, 0.0, 0.25 * parity * np.cos(angle) / denom).astype(np.float32)
    high = smat.astype(ml_dtypes.bfloat16)
    low = (smat - high.astype(np.float32)).astype(ml_dtypes.bfloat16)
    blocks = []
    for me in range(inst_count):
        for hop in range(inst_count):
            other = (me - hop) % inst_count
            rows = []
            for part in (high, low):
                cut = part[other * inst_dev : (other + 1) * inst_dev, me * inst_dev : (me + 1) * inst_dev]
                wide = np.kron(np.eye(VARS, dtype=np.float32), cut.T.astype(np.float32))
                rows.append(np.concatenate([wide, wide], axis=1))
            blocks.append(np.concatenate(rows, axis=0))
    side = 2 * VARS * inst_dev
    stacked = np.stack(blocks).reshape(inst_count, inst_count, side, side)
    return jnp.asarray(stacked.astype(ml_dtypes.bfloat16))


def split_parts(value):
    high = value.astype(jnp.bfloat16)
    low = (value - high.astype(jnp.float32)).astype(jnp.bfloat16)
    return high, low


def step_kernel(
    ninst,
    npeer,
    adj_hbm,
    src_hbm,
    diag_hbm,
    face_hbm,
    nbr_ref,
    dtau_ref,
    fsrc_ref,
    fwt_ref,
    cnt_ref,
    fdst_ref,
    spec_ref,
    out_ref,
    adj,
    source,
    diag,
    facej,
    parts,
    far,
    far_parts,
    near,
    faced,
    total,
    slots,
    coefs,
    packs,
    landed,
    values,
    place,
    load_sem,
    far_send,
    far_recv,
    fr_send,
    fr_recv,
):
    rows, cells = adj.shape
    idev = rows // VARS
    tiles = cells // TILE
    half = rows // 2
    pairs = npeer // 2
    cap = TILE // 2
    strip = tiles * FACES
    my_inst = lax.axis_index("inst")
    my_cell = lax.axis_index("cell")

    loads = [
        pltpu.make_async_copy(adj_hbm, adj, load_sem.at[0]),
        pltpu.make_async_copy(face_hbm, facej, load_sem.at[1]),
        pltpu.make_async_copy(diag_hbm, diag, load_sem.at[2]),
        pltpu.make_async_copy(src_hbm, source, load_sem.at[3]),
    ]
    for load in loads:
        load.start()

    barrier = pltpu.get_barrier_semaphore()
    for hop in range(1, ninst):
        pl.semaphore_signal(
            barrier, inc=1, device_id=(lax.rem(my_inst + hop, ninst), my_cell), device_id_type=MESH
        )
    for hop in range(1, npeer):
        pl.semaphore_signal(
            barrier, inc=1, device_id=(my_inst, lax.rem(my_cell + hop, npeer)), device_id_type=MESH
        )

    lane = lax.broadcasted_iota(jnp.int32, (1, TILE), 1)
    low_half = lane < cap
    slots[...] = jnp.concatenate([fsrc_ref[0:pairs, :], fsrc_ref[pairs:npeer, :]], axis=1)
    coefs[...] = jnp.concatenate([fwt_ref[0:pairs, :], fwt_ref[pairs:npeer, :]], axis=1)
    loads[0].wait()
    high, low = split_parts(adj[...])
    parts[0:rows, :] = high
    parts[rows:, :] = low

    pl.semaphore_wait(barrier, ninst + npeer - 2)
    far_copies = []
    for hop in range(1, ninst):
        copy = pltpu.make_async_remote_copy(
            src_ref=adj,
            dst_ref=far.at[hop - 1],
            send_sem=far_send.at[hop - 1],
            recv_sem=far_recv.at[hop - 1],
            device_id=(lax.rem(my_inst + hop, ninst), my_cell),
            device_id_type=MESH,
        )
        copy.start()
        far_copies.append(copy)

    def fringe_copy(peer, hop):
        return pltpu.make_async_remote_copy(
            src_ref=packs.at[peer],
            dst_ref=landed.at[my_cell],
            send_sem=fr_send.at[hop],
            recv_sem=fr_recv.at[hop],
            device_id=(my_inst, peer),
            device_id_type=MESH,
        )

    cell_rows = lax.broadcasted_iota(jnp.int32, (cells, 2 * TILE), 0)
    wide_low = jnp.broadcast_to(low_half, (half, TILE))
    place_of = lax.rem(lane, cap)
    steps = pairs // 2
    for step in range(steps):
        first = 2 * lax.rem(my_cell // 2 + step, steps)
        picked_slots = jnp.concatenate(
            [slots[pl.ds(first, 1), :], slots[pl.ds(first + 1, 1), :]], axis=1
        )
        select = jnp.where(cell_rows == picked_slots, 1.0, 0.0).astype(jnp.bfloat16)
        both = jnp.dot(parts[...], select, preferred_element_type=jnp.float32)
        picked = both[0:rows, :] + both[rows:, :]
        for sub in range(2):
            pair = first + sub
            live = place_of < jnp.where(low_half, cnt_ref[0, pair], cnt_ref[0, pair + pairs])
            coef = jnp.where(live, coefs[pl.ds(pair, 1), :], 0.0)
            block = picked[:, sub * TILE : (sub + 1) * TILE] * coef
            upper, lower = block[0:half, :], block[half:, :]
            packs[pair] = jnp.where(wide_low, upper, pltpu.roll(lower, cap, 1))
            packs[pair + pairs] = jnp.where(wide_low, pltpu.roll(upper, cap, 1), lower)
            for peer in (pair, pair + pairs):
                hop = lax.rem(peer - my_cell + npeer, npeer)

                @pl.when(hop != 0)
                def _():
                    fringe_copy(peer, hop).start()

    landed[my_cell] = packs[my_cell]

    for tile in range(tiles):
        for face in range(FACES):
            other = nbr_ref[face, tile]
            for var in range(VARS):
                span = slice(var * idev, (var + 1) * idev)
                value = adj[span, 0:TILE]
                for cand in range(1, tiles):
                    value = jnp.where(other == cand, adj[span, cand * TILE : (cand + 1) * TILE], value)
                at = var * idev * strip + tile * FACES + face
                near[pl.ds(at, idev, stride=strip), :] = value

    cell_ids = lax.broadcasted_iota(jnp.int32, (cells, TILE), 0)
    for pair in range(pairs):
        donors = jnp.concatenate([fdst_ref[pair], fdst_ref[pair + pairs]], axis=1)
        hit = jnp.where(cell_ids == donors, 1.0, 0.0).astype(jnp.bfloat16)
        place[:, pair * TILE : (pair + 1) * TILE] = hit

    loads[1].wait()

    def one_instance(inst, carry):
        sums = [jnp.zeros((strip, TILE), jnp.float32) for _ in range(VARS)]
        for var in range(VARS):
            start = pl.multiple_of((var * idev + inst) * strip, strip)
            beside = near[pl.ds(start, strip), :]
            for eqn in range(VARS):
                sums[eqn] = sums[eqn] + facej[inst, var, eqn].astype(jnp.float32) * beside
        for eqn in range(VARS):
            start = pl.multiple_of((eqn * idev + inst) * strip, strip)
            faced[pl.ds(start, strip), :] = sums[eqn]
        return carry

    lax.fori_loop(0, idev, one_instance, 0)

    both = jnp.dot(spec_ref[my_inst, 0], parts[...], preferred_element_type=jnp.float32)
    total[...] = both[0:rows, :] + both[rows:, :]
    loads[2].wait()
    loads[3].wait()
    for tile in range(tiles):
        cols = slice(tile * TILE, (tile + 1) * TILE)
        mine = [adj[var * idev : (var + 1) * idev, cols] for var in range(VARS)]
        for eqn in range(VARS):
            span = slice(eqn * idev, (eqn + 1) * idev)
            value = total[span, cols] - source[span, cols]
            for var in range(VARS):
                value = value + diag[var, eqn, :, cols].astype(jnp.float32) * mine[var]
            for face in range(FACES):
                at = eqn * idev * strip + tile * FACES + face
                value = value + faced[pl.ds(at, idev, stride=strip), :]
            total[span, cols] = value

    for hop in range(1, ninst):
        far_copies[hop - 1].wait_recv()
        high, low = split_parts(far[hop - 1])
        far_parts[0:rows, :] = high
        far_parts[rows:, :] = low
        both = jnp.dot(spec_ref[my_inst, hop], far_parts[...], preferred_element_type=jnp.float32)
        total[...] += both[0:rows, :] + both[rows:, :]

    for hop in range(1, npeer):
        fringe_copy(lax.rem(my_cell + hop, npeer), hop).wait_recv()
    for pair in range(pairs):
        one, two = landed[pair], landed[pair + pairs]
        cols = slice(pair * TILE, (pair + 1) * TILE)
        high, low = split_parts(jnp.where(wide_low, one, pltpu.roll(two, cap, 1)))
        values[0:half, cols] = high
        values[rows : rows + half, cols] = low
        high, low = split_parts(jnp.where(wide_low, pltpu.roll(one, cap, 1), two))
        values[half:rows, cols] = high
        values[rows + half :, cols] = low
    for chunk in range(cells // 256):
        both = lax.dot_general(
            values[...],
            place[chunk * 256 : (chunk + 1) * 256, :],
            (((1,), (1,)), ((), ())),
            preferred_element_type=jnp.float32,
        )
        fringe = both[0:rows, :] + both[rows:, :]
        for sub in range(2):
            tile = chunk * 2 + sub
            cols = slice(tile * TILE, (tile + 1) * TILE)
            whole = total[:, cols] + fringe[:, sub * TILE : (sub + 1) * TILE]
            out_ref[:, cols] = adj[:, cols] - dtau_ref[tile : tile + 1, :] * whole

    for copy in far_copies:
        copy.wait_send()
    for hop in range(1, npeer):
        fringe_copy(lax.rem(my_cell + hop, npeer), hop).wait_send()


def fused_step(
    ninst,
    npeer,
    adjoint,
    source,
    jac_diag,
    jac_face,
    tile_nbr,
    dtau,
    fringe_src,
    fringe_wt,
    fringe_count,
    fringe_dst,
):
    idev, nvars, cells = adjoint.shape
    tiles = cells // TILE
    rows = idev * nvars
    pairs = npeer // 2
    strip = tiles * FACES
    adj = jnp.transpose(adjoint, (1, 0, 2)).reshape(rows, cells)
    src = jnp.transpose(source, (1, 0, 2)).reshape(rows, cells)
    diag = jnp.transpose(jac_diag, (1, 2, 0, 3))
    face = jac_face.reshape(idev, FACES, nvars, nvars, tiles, TILE)
    face = jnp.transpose(face, (0, 2, 3, 4, 1, 5)).reshape(idev, nvars, nvars, strip, TILE)
    anywhere = pl.BlockSpec(memory_space=pltpu.HBM)
    vmem = pl.BlockSpec(memory_space=pltpu.VMEM)
    smem = pl.BlockSpec(memory_space=pltpu.SMEM)
    out = pl.pallas_call(
        functools.partial(step_kernel, ninst, npeer),
        out_shape=jax.ShapeDtypeStruct((rows, cells), jnp.float32),
        in_specs=[anywhere] * 4 + [smem, vmem, vmem, vmem, smem, vmem, vmem],
        out_specs=vmem,
        scratch_shapes=[
            pltpu.VMEM((rows, cells), jnp.float32),
            pltpu.VMEM((rows, cells), jnp.float32),
            pltpu.VMEM((nvars, nvars, idev, cells), jnp.bfloat16),
            pltpu.VMEM((idev, nvars, nvars, strip, TILE), jnp.bfloat16),
            pltpu.VMEM((2 * rows, cells), jnp.bfloat16),
            pltpu.VMEM((ninst - 1, rows, cells), jnp.float32),
            pltpu.VMEM((2 * rows, cells), jnp.bfloat16),
            pltpu.VMEM((rows * strip, TILE), jnp.float32),
            pltpu.VMEM((rows * strip, TILE), jnp.float32),
            pltpu.VMEM((rows, cells), jnp.float32),
            pltpu.VMEM((pairs, TILE), jnp.int32),
            pltpu.VMEM((pairs, TILE), jnp.float32),
            pltpu.VMEM((npeer, rows // 2, TILE), jnp.float32),
            pltpu.VMEM((npeer, rows // 2, TILE), jnp.float32),
            pltpu.VMEM((2 * rows, pairs * TILE), jnp.bfloat16),
            pltpu.VMEM((cells, pairs * TILE), jnp.bfloat16),
            pltpu.SemaphoreType.DMA((4,)),
            pltpu.SemaphoreType.DMA((ninst - 1,)),
            pltpu.SemaphoreType.DMA((ninst - 1,)),
            pltpu.SemaphoreType.DMA((npeer,)),
            pltpu.SemaphoreType.DMA((npeer,)),
        ],
        compiler_params=pltpu.CompilerParams(
            collective_id=0, has_side_effects=True, vmem_limit_bytes=56 * 1024 * 1024
        ),
    )(
        adj,
        src,
        diag,
        face,
        tile_nbr.T,
        dtau.reshape(tiles, TILE),
        fringe_src[0],
        fringe_wt[0],
        fringe_count,
        fringe_dst,
        spectral_blocks(ninst, idev),
    )
    return jnp.transpose(out.reshape(nvars, idev, cells), (1, 0, 2))


def solution(mesh):
    placed = (
        P("inst", None, "cell"),
        P("inst", None, "cell"),
        P("inst", None, None, "cell"),
        P("inst", None, None, None, "cell"),
        P("cell", None),
        P("cell"),
        P("cell", None, None),
        P("cell", None, None),
        P("cell", None),
        P(None, "cell", None),
    )
    ninst, npeer = mesh.shape["inst"], mesh.shape["cell"]

    def body(adjoint, *rest):
        idev, _, cells = adjoint.shape
        slot_cap = rest[5].shape[2]
        fits = idev % 8 == 0 and ninst > 1 and npeer % 4 == 0
        if fits and cells % 256 == 0 and slot_cap * 2 == TILE:
            return fused_step(ninst, npeer, adjoint, *rest)
        return on_device(adjoint, *rest)

    return jax.shard_map(
        body, mesh=mesh, in_specs=placed, out_specs=P("inst", None, "cell"), check_vma=False
    )
```

```python
import functools
import math

import jax
import jax.numpy as jnp
import ml_dtypes
import numpy as np
from jax import lax
from jax.experimental import pallas as pl
from jax.experimental.pallas import tpu as pltpu
from jax.sharding import PartitionSpec as P

INSTANCES = 16
FACES = 4
TILE = 128
VARS = 6
MESH = pl.DeviceIdType.MESH


def spectral_matrix(count):
    rows = jnp.arange(count, dtype=jnp.int32)[:, None]
    cols = jnp.arange(count, dtype=jnp.int32)[None, :]
    offset = rows - cols
    angle = offset.astype(jnp.float32) * (jnp.pi / count)
    parity = jnp.where(offset % 2 == 0, 1.0, -1.0).astype(jnp.float32)
    denom = jnp.where(offset == 0, 1.0, jnp.sin(angle))
    value = 0.25 * parity * jnp.cos(angle) / denom
    return jnp.where(offset == 0, 0.0, value)


def pick_rows(flat, sources, weights, block):
    cells_dev = flat.shape[1]
    nblocks = sources.shape[0] // block
    cell_ids = jnp.arange(cells_dev, dtype=jnp.int32)[:, None]

    def one_block(pair):
        index_block, weight_block = pair
        select = jnp.where(cell_ids == index_block[None, :], weight_block[None, :], 0.0)
        return jnp.dot(
            flat, select, precision=lax.Precision.HIGHEST, preferred_element_type=jnp.float32
        )

    result = lax.map(one_block, (sources.reshape(nblocks, block), weights.reshape(nblocks, block)))
    return jnp.transpose(result, (1, 0, 2)).reshape(flat.shape[0], -1)


def place_rows(values, targets, cells_dev, block):
    nblocks = targets.shape[0] // block
    cell_ids = jnp.arange(cells_dev, dtype=jnp.int32)[None, :]

    def add_block(step, total):
        start = step * block
        target_block = lax.dynamic_slice_in_dim(targets, start, block, 0)
        value_block = lax.dynamic_slice_in_dim(values, start, block, 1)
        select = jnp.where(target_block[:, None] == cell_ids, 1.0, 0.0).astype(jnp.float32)
        return total + jnp.dot(
            value_block, select, precision=lax.Precision.HIGHEST, preferred_element_type=jnp.float32
        )

    empty = jnp.zeros((values.shape[0], cells_dev), jnp.float32)
    return lax.fori_loop(0, nblocks, add_block, empty)


def on_device(
    adjoint,
    source,
    jac_diag,
    jac_face,
    tile_nbr,
    dtau,
    fringe_src,
    fringe_wt,
    fringe_count,
    fringe_dst,
):
    inst_dev, nvars, cells_dev = adjoint.shape
    tiles_dev = cells_dev // TILE
    peer_count, slot_cap = (fringe_wt.shape[1], fringe_wt.shape[2])
    total_slots = peer_count * slot_cap
    block = math.gcd(total_slots, 512)
    smat = spectral_matrix(INSTANCES)
    flat = adjoint.reshape(inst_dev * nvars, cells_dev)
    live = jnp.arange(slot_cap, dtype=jnp.int32)[None, :] < fringe_count[0][:, None]
    coef = jnp.where(live, fringe_wt[0], 0.0).reshape(-1)
    picked = pick_rows(flat, fringe_src[0].reshape(-1), coef, block)
    outgoing = picked.reshape(inst_dev, nvars, peer_count, slot_cap)
    arrived = lax.all_to_all(outgoing, "cell", split_axis=2, concat_axis=2, tiled=True)
    spread = lax.all_to_all(adjoint, "inst", split_axis=2, concat_axis=0, tiled=True)
    mixed = jnp.einsum("ji,jac->iac", smat, spread, precision=lax.Precision.HIGHEST)
    temporal = lax.all_to_all(mixed, "inst", split_axis=0, concat_axis=2, tiled=True)
    own = jnp.sum(jac_diag.astype(jnp.float32) * adjoint[:, :, None, :], axis=1)
    tiles = adjoint.reshape(inst_dev, nvars, tiles_dev, TILE)
    tile_ids = jnp.arange(tiles_dev, dtype=jnp.int32)[None, :]
    faced = jnp.zeros_like(adjoint)
    for face in range(FACES):
        select = jnp.where(tile_nbr[:, face][:, None] == tile_ids, 1.0, 0.0).astype(jnp.float32)
        near = jnp.einsum("tu,iaup->iatp", select, tiles, precision=lax.Precision.HIGHEST)
        near = near.reshape(inst_dev, nvars, cells_dev)
        faced = faced + jnp.sum(jac_face[:, face].astype(jnp.float32) * near[:, :, None, :], axis=1)
    donors = fringe_dst[:, 0, :].reshape(-1)
    fringe = place_rows(arrived.reshape(inst_dev * nvars, -1), donors, cells_dev, block)
    fringe = fringe.reshape(inst_dev, nvars, cells_dev)
    total = own + faced + temporal + fringe - source
    return adjoint - dtau[None, None, :] * total


def spectral_blocks(inst_count, inst_dev):
    offset = np.arange(INSTANCES)[:, None] - np.arange(INSTANCES)[None, :]
    angle = offset * (np.pi / INSTANCES)
    parity = np.where(offset % 2 == 0, 1.0, -1.0)
    denom = np.where(offset == 0, 1.0, np.sin(angle))
    smat = np.where(offset == 0, 0.0, 0.25 * parity * np.cos(angle) / denom).astype(np.float32)
    high = smat.astype(ml_dtypes.bfloat16)
    low = (smat - high.astype(np.float32)).astype(ml_dtypes.bfloat16)
    blocks = []
    for me in range(inst_count):
        for hop in range(inst_count):
            other = (me - hop) % inst_count
            rows = []
            for part in (high, low):
                cut = part[other * inst_dev : (other + 1) * inst_dev, me * inst_dev : (me + 1) * inst_dev]
                wide = np.kron(np.eye(VARS, dtype=np.float32), cut.T.astype(np.float32))
                rows.append(np.concatenate([wide, wide], axis=1))
            blocks.append(np.concatenate(rows, axis=0))
    side = 2 * VARS * inst_dev
    stacked = np.stack(blocks).reshape(inst_count, inst_count, side, side)
    return jnp.asarray(stacked.astype(ml_dtypes.bfloat16))


def split_parts(value):
    high = value.astype(jnp.bfloat16)
    low = (value - high.astype(jnp.float32)).astype(jnp.bfloat16)
    return high, low


def step_kernel(
    ninst,
    npeer,
    adj_hbm,
    fsrc_hbm,
    fwt_hbm,
    cnt_hbm,
    nbr_hbm,
    fdst_hbm,
    face_hbm,
    diag_hbm,
    src_hbm,
    spec_hbm,
    dtau_hbm,
    out_ref,
    adj,
    fsrc,
    fwt,
    cnt,
    nbr,
    fdst,
    facej,
    diag,
    source,
    spec,
    dtau,
    parts,
    far,
    far_parts,
    near,
    faced,
    total,
    slots,
    coefs,
    packs,
    landed,
    values,
    place,
    load_sem,
    far_send,
    far_recv,
    fr_send,
    fr_recv,
):
    rows, cells = adj.shape
    idev = rows // VARS
    tiles = cells // TILE
    half = rows // 2
    pairs = npeer // 2
    cap = TILE // 2
    strip = tiles * FACES
    steps = pairs // 2
    my_inst = lax.axis_index("inst")
    my_cell = lax.axis_index("cell")

    ends = [
        (adj_hbm, adj),
        (fsrc_hbm, fsrc),
        (fwt_hbm, fwt),
        (cnt_hbm, cnt),
        (nbr_hbm, nbr),
        (fdst_hbm, fdst),
        (face_hbm, facej),
        (diag_hbm, diag),
        (src_hbm, source),
        (spec_hbm.at[my_inst], spec),
        (dtau_hbm, dtau),
    ]
    loads = [pltpu.make_async_copy(one, two, load_sem.at[at]) for at, (one, two) in enumerate(ends)]
    for load in loads[:4]:
        load.start()
    barrier = pltpu.get_barrier_semaphore()
    for hop in range(1, ninst):
        pl.semaphore_signal(
            barrier, inc=1, device_id=(lax.rem(my_inst + hop, ninst), my_cell), device_id_type=MESH
        )
    for hop in range(1, npeer):
        pl.semaphore_signal(
            barrier, inc=1, device_id=(my_inst, lax.rem(my_cell + hop, npeer)), device_id_type=MESH
        )
    for load in loads[4:]:
        load.start()

    lane = lax.broadcasted_iota(jnp.int32, (npeer, cap), 1)
    diagonal = lax.broadcasted_iota(jnp.int32, (npeer, npeer), 0) == lax.broadcasted_iota(
        jnp.int32, (npeer, npeer), 1
    )
    wide_low = lax.broadcasted_iota(jnp.int32, (half, TILE), 1) < cap
    window = lax.broadcasted_iota(jnp.int32, (256, 256), 0).astype(jnp.float32).astype(jnp.bfloat16)
    one, zero = jnp.bfloat16(1.0), jnp.bfloat16(0.0)

    def window_hits(ids, at):
        return jnp.where(window == (ids - 256 * at).astype(jnp.float32).astype(jnp.bfloat16), one, zero)

    for load in loads[1:4]:
        load.wait()
    slots[...] = jnp.concatenate([fsrc[0:pairs, :], fsrc[pairs:npeer, :]], axis=1)
    live_count = jnp.sum(
        jnp.where(diagonal, jnp.broadcast_to(cnt[...], (npeer, npeer)).astype(jnp.float32), 0.0), axis=1, keepdims=True
    )
    coef = jnp.where(lane.astype(jnp.float32) < live_count, fwt[...], 0.0)
    coefs[...] = jnp.concatenate([coef[0:pairs, :], coef[pairs:npeer, :]], axis=1)
    loads[0].wait()
    high, low = split_parts(adj[...])
    parts[0:rows, :] = high
    parts[rows:, :] = low

    def fringe_copy(peer, hop):
        return pltpu.make_async_remote_copy(
            src_ref=packs.at[peer],
            dst_ref=landed.at[my_cell],
            send_sem=fr_send.at[hop],
            recv_sem=fr_recv.at[hop],
            device_id=(my_inst, peer),
            device_id_type=MESH,
        )

    def pick_step(step):
        first = 2 * lax.rem(my_cell // 2 + step, steps)
        ids = jnp.concatenate([slots[pl.ds(first, 1), :], slots[pl.ds(first + 1, 1), :]], axis=1)
        both = jnp.zeros((2 * rows, 256), jnp.float32)
        for at in range(cells // 256):
            both = both + jnp.dot(
                parts[:, at * 256 : (at + 1) * 256],
                window_hits(ids, at),
                preferred_element_type=jnp.float32,
            )
        picked = both[0:rows, :] + both[rows:, :]
        for sub in range(2):
            pair = first + sub
            block = picked[:, sub * TILE : (sub + 1) * TILE] * coefs[pl.ds(pair, 1), :]
            upper, lower = block[0:half, :], block[half:, :]
            packs[pair] = jnp.where(wide_low, upper, pltpu.roll(lower, cap, 1))
            packs[pair + pairs] = jnp.where(wide_low, pltpu.roll(upper, cap, 1), lower)

    def send_step(step):
        first = 2 * lax.rem(my_cell // 2 + step, steps)
        for peer in (first + pairs, first + pairs + 1, first, first + 1):
            hop = lax.rem(peer - my_cell + npeer, npeer)

            @pl.when(hop != 0)
            def _():
                fringe_copy(peer, hop).start()

    early = steps // 2
    for step in range(early):
        pick_step(step)
    pl.semaphore_wait(barrier, ninst + npeer - 2)
    far_copies = []
    for hop in range(1, ninst):
        copy = pltpu.make_async_remote_copy(
            src_ref=adj,
            dst_ref=far.at[hop - 1],
            send_sem=far_send.at[hop - 1],
            recv_sem=far_recv.at[hop - 1],
            device_id=(lax.rem(my_inst + hop, ninst), my_cell),
            device_id_type=MESH,
        )
        copy.start()
        far_copies.append(copy)
    for step in range(early):
        send_step(step)
    for step in range(early, steps):
        pick_step(step)
        send_step(step)
    landed[my_cell] = packs[my_cell]

    loads[4].wait()
    for tile in range(tiles):
        for face in range(FACES):
            other = jnp.broadcast_to(nbr[face : face + 1, tile : tile + 1], (idev, TILE))
            picks = [other == cand for cand in range(1, tiles)]
            for var in range(VARS):
                span = slice(var * idev, (var + 1) * idev)
                value = adj[span, 0:TILE]
                for cand in range(1, tiles):
                    value = jnp.where(picks[cand - 1], adj[span, cand * TILE : (cand + 1) * TILE], value)
                at = var * idev * strip + tile * FACES + face
                near[pl.ds(at, idev, stride=strip), :] = value

    loads[6].wait()

    def one_instance(inst, carry):
        sums = [jnp.zeros((strip, TILE), jnp.float32) for _ in range(VARS)]
        for var in range(VARS):
            start = pl.multiple_of((var * idev + inst) * strip, strip)
            beside = near[pl.ds(start, strip), :]
            for eqn in range(VARS):
                sums[eqn] = sums[eqn] + facej[inst, var, eqn].astype(jnp.float32) * beside
        for eqn in range(VARS):
            start = pl.multiple_of((eqn * idev + inst) * strip, strip)
            faced[pl.ds(start, strip), :] = sums[eqn]
        return carry

    lax.fori_loop(0, idev, one_instance, 0)

    for load in loads[7:10]:
        load.wait()
    both = jnp.dot(spec[0], parts[...], preferred_element_type=jnp.float32)
    total[...] = both[0:rows, :] + both[rows:, :]
    for tile in range(tiles):
        cols = slice(tile * TILE, (tile + 1) * TILE)
        mine = [adj[var * idev : (var + 1) * idev, cols] for var in range(VARS)]
        for eqn in range(VARS):
            span = slice(eqn * idev, (eqn + 1) * idev)
            value = total[span, cols] - source[span, cols]
            for var in range(VARS):
                value = value + diag[var, eqn, :, cols].astype(jnp.float32) * mine[var]
            for face in range(FACES):
                at = eqn * idev * strip + tile * FACES + face
                value = value + faced[pl.ds(at, idev, stride=strip), :]
            total[span, cols] = value

    loads[5].wait()
    loads[10].wait()
    for group in range(steps):
        pair = 2 * group
        ids = jnp.concatenate(
            [fdst[pair], fdst[pair + pairs], fdst[pair + 1], fdst[pair + 1 + pairs]], axis=1
        )
        for at in range(cells // 256):
            place[group, at * 256 : (at + 1) * 256, :] = window_hits(ids, at)

    def take_step(step):
        group = lax.rem(my_cell // 2 - step + steps, steps)
        first = 2 * group
        for origin in (first, first + 1, first + pairs, first + pairs + 1):
            hop = lax.rem(my_cell - origin + npeer, npeer)

            @pl.when(hop != 0)
            def _():
                fringe_copy(lax.rem(my_cell + hop, npeer), hop).wait_recv()

        for sub in range(2):
            here, there = landed[first + sub], landed[first + sub + pairs]
            cols = slice(sub * TILE, (sub + 1) * TILE)
            high, low = split_parts(jnp.where(wide_low, here, pltpu.roll(there, cap, 1)))
            values[0:half, cols] = high
            values[rows : rows + half, cols] = low
            high, low = split_parts(jnp.where(wide_low, pltpu.roll(here, cap, 1), there))
            values[half:rows, cols] = high
            values[rows + half :, cols] = low
        for at in range(cells // 256):
            both = lax.dot_general(
                values[...],
                place[group, at * 256 : (at + 1) * 256, :],
                (((1,), (1,)), ((), ())),
                preferred_element_type=jnp.float32,
            )
            fringe = both[0:rows, :] + both[rows:, :]
            for sub in range(2):
                tile = at * 2 + sub
                cols = slice(tile * TILE, (tile + 1) * TILE)
                whole = total[:, cols] + fringe[:, sub * TILE : (sub + 1) * TILE]
                if step < steps - 1:
                    total[:, cols] = whole
                else:
                    out_ref[:, cols] = adj[:, cols] - dtau[tile : tile + 1, :] * whole

    for step in range(early):
        take_step(step)
    for hop in range(1, ninst):
        far_copies[hop - 1].wait_recv()
        high, low = split_parts(far[hop - 1])
        far_parts[0:rows, :] = high
        far_parts[rows:, :] = low
        both = jnp.dot(spec[hop], far_parts[...], preferred_element_type=jnp.float32)
        total[...] += both[0:rows, :] + both[rows:, :]
    for step in range(early, steps):
        take_step(step)

    for copy in far_copies:
        copy.wait_send()
    for hop in range(1, npeer):
        fringe_copy(lax.rem(my_cell + hop, npeer), hop).wait_send()


def fused_step(
    ninst,
    npeer,
    adjoint,
    source,
    jac_diag,
    jac_face,
    tile_nbr,
    dtau,
    fringe_src,
    fringe_wt,
    fringe_count,
    fringe_dst,
):
    idev, nvars, cells = adjoint.shape
    tiles = cells // TILE
    rows = idev * nvars
    pairs = npeer // 2
    strip = tiles * FACES
    adj = jnp.transpose(adjoint, (1, 0, 2)).reshape(rows, cells)
    src = jnp.transpose(source, (1, 0, 2)).reshape(rows, cells)
    diag = jnp.transpose(jac_diag, (1, 2, 0, 3))
    face = jac_face.reshape(idev, FACES, nvars, nvars, tiles, TILE)
    face = jnp.transpose(face, (0, 2, 3, 4, 1, 5)).reshape(idev, nvars, nvars, strip, TILE)
    spectral = spectral_blocks(ninst, idev)
    operands = [
        adj,
        fringe_src[0],
        fringe_wt[0],
        fringe_count,
        tile_nbr.T,
        fringe_dst,
        face,
        diag,
        src,
        spectral,
        dtau.reshape(tiles, TILE),
    ]
    held = [pltpu.VMEM(one.shape, one.dtype) for one in operands]
    held[9] = pltpu.VMEM(spectral.shape[1:], spectral.dtype)
    out = pl.pallas_call(
        functools.partial(step_kernel, ninst, npeer),
        out_shape=jax.ShapeDtypeStruct((rows, cells), jnp.float32),
        in_specs=[pl.BlockSpec(memory_space=pltpu.HBM)] * len(operands),
        out_specs=pl.BlockSpec(memory_space=pltpu.VMEM),
        scratch_shapes=held
        + [
            pltpu.VMEM((2 * rows, cells), jnp.bfloat16),
            pltpu.VMEM((ninst - 1, rows, cells), jnp.float32),
            pltpu.VMEM((2 * rows, cells), jnp.bfloat16),
            pltpu.VMEM((rows * strip, TILE), jnp.float32),
            pltpu.VMEM((rows * strip, TILE), jnp.float32),
            pltpu.VMEM((rows, cells), jnp.float32),
            pltpu.VMEM((pairs, TILE), jnp.int32),
            pltpu.VMEM((pairs, TILE), jnp.float32),
            pltpu.VMEM((npeer, rows // 2, TILE), jnp.float32),
            pltpu.VMEM((npeer, rows // 2, TILE), jnp.float32),
            pltpu.VMEM((2 * rows, 256), jnp.bfloat16),
            pltpu.VMEM((pairs // 2, cells, 256), jnp.bfloat16),
            pltpu.SemaphoreType.DMA((len(operands),)),
            pltpu.SemaphoreType.DMA((ninst - 1,)),
            pltpu.SemaphoreType.DMA((ninst - 1,)),
            pltpu.SemaphoreType.DMA((npeer,)),
            pltpu.SemaphoreType.DMA((npeer,)),
        ],
        compiler_params=pltpu.CompilerParams(
            collective_id=0, has_side_effects=True, vmem_limit_bytes=56 * 1024 * 1024
        ),
    )(*operands)
    return jnp.transpose(out.reshape(nvars, idev, cells), (1, 0, 2))


def solution(mesh):
    placed = (
        P("inst", None, "cell"),
        P("inst", None, "cell"),
        P("inst", None, None, "cell"),
        P("inst", None, None, None, "cell"),
        P("cell", None),
        P("cell"),
        P("cell", None, None),
        P("cell", None, None),
        P("cell", None),
        P(None, "cell", None),
    )
    ninst, npeer = mesh.shape["inst"], mesh.shape["cell"]

    def body(adjoint, *rest):
        idev, _, cells = adjoint.shape
        slot_cap = rest[5].shape[2]
        fits = idev % 8 == 0 and ninst > 1 and npeer % 4 == 0
        if fits and cells % 256 == 0 and slot_cap * 2 == TILE:
            return fused_step(ninst, npeer, adjoint, *rest)
        return on_device(adjoint, *rest)

    return jax.shard_map(
        body, mesh=mesh, in_specs=placed, out_specs=P("inst", None, "cell"), check_vma=False
    )
```

```python
import functools
import math

import jax
import jax.numpy as jnp
import ml_dtypes
import numpy as np
from jax import lax
from jax.experimental import pallas as pl
from jax.experimental.pallas import tpu as pltpu
from jax.sharding import PartitionSpec as P

INSTANCES = 16
FACES = 4
TILE = 128
VARS = 6
MESH = pl.DeviceIdType.MESH


def spectral_matrix(count):
    rows = jnp.arange(count, dtype=jnp.int32)[:, None]
    cols = jnp.arange(count, dtype=jnp.int32)[None, :]
    offset = rows - cols
    angle = offset.astype(jnp.float32) * (jnp.pi / count)
    parity = jnp.where(offset % 2 == 0, 1.0, -1.0).astype(jnp.float32)
    denom = jnp.where(offset == 0, 1.0, jnp.sin(angle))
    value = 0.25 * parity * jnp.cos(angle) / denom
    return jnp.where(offset == 0, 0.0, value)


def pick_rows(flat, sources, weights, block):
    cells_dev = flat.shape[1]
    nblocks = sources.shape[0] // block
    cell_ids = jnp.arange(cells_dev, dtype=jnp.int32)[:, None]

    def one_block(pair):
        index_block, weight_block = pair
        select = jnp.where(cell_ids == index_block[None, :], weight_block[None, :], 0.0)
        return jnp.dot(
            flat, select, precision=lax.Precision.HIGHEST, preferred_element_type=jnp.float32
        )

    result = lax.map(one_block, (sources.reshape(nblocks, block), weights.reshape(nblocks, block)))
    return jnp.transpose(result, (1, 0, 2)).reshape(flat.shape[0], -1)


def place_rows(values, targets, cells_dev, block):
    nblocks = targets.shape[0] // block
    cell_ids = jnp.arange(cells_dev, dtype=jnp.int32)[None, :]

    def add_block(step, total):
        start = step * block
        target_block = lax.dynamic_slice_in_dim(targets, start, block, 0)
        value_block = lax.dynamic_slice_in_dim(values, start, block, 1)
        select = jnp.where(target_block[:, None] == cell_ids, 1.0, 0.0).astype(jnp.float32)
        return total + jnp.dot(
            value_block, select, precision=lax.Precision.HIGHEST, preferred_element_type=jnp.float32
        )

    empty = jnp.zeros((values.shape[0], cells_dev), jnp.float32)
    return lax.fori_loop(0, nblocks, add_block, empty)


def on_device(
    adjoint,
    source,
    jac_diag,
    jac_face,
    tile_nbr,
    dtau,
    fringe_src,
    fringe_wt,
    fringe_count,
    fringe_dst,
):
    inst_dev, nvars, cells_dev = adjoint.shape
    tiles_dev = cells_dev // TILE
    peer_count, slot_cap = (fringe_wt.shape[1], fringe_wt.shape[2])
    total_slots = peer_count * slot_cap
    block = math.gcd(total_slots, 512)
    smat = spectral_matrix(INSTANCES)
    flat = adjoint.reshape(inst_dev * nvars, cells_dev)
    live = jnp.arange(slot_cap, dtype=jnp.int32)[None, :] < fringe_count[0][:, None]
    coef = jnp.where(live, fringe_wt[0], 0.0).reshape(-1)
    picked = pick_rows(flat, fringe_src[0].reshape(-1), coef, block)
    outgoing = picked.reshape(inst_dev, nvars, peer_count, slot_cap)
    arrived = lax.all_to_all(outgoing, "cell", split_axis=2, concat_axis=2, tiled=True)
    spread = lax.all_to_all(adjoint, "inst", split_axis=2, concat_axis=0, tiled=True)
    mixed = jnp.einsum("ji,jac->iac", smat, spread, precision=lax.Precision.HIGHEST)
    temporal = lax.all_to_all(mixed, "inst", split_axis=0, concat_axis=2, tiled=True)
    own = jnp.sum(jac_diag.astype(jnp.float32) * adjoint[:, :, None, :], axis=1)
    tiles = adjoint.reshape(inst_dev, nvars, tiles_dev, TILE)
    tile_ids = jnp.arange(tiles_dev, dtype=jnp.int32)[None, :]
    faced = jnp.zeros_like(adjoint)
    for face in range(FACES):
        select = jnp.where(tile_nbr[:, face][:, None] == tile_ids, 1.0, 0.0).astype(jnp.float32)
        near = jnp.einsum("tu,iaup->iatp", select, tiles, precision=lax.Precision.HIGHEST)
        near = near.reshape(inst_dev, nvars, cells_dev)
        faced = faced + jnp.sum(jac_face[:, face].astype(jnp.float32) * near[:, :, None, :], axis=1)
    donors = fringe_dst[:, 0, :].reshape(-1)
    fringe = place_rows(arrived.reshape(inst_dev * nvars, -1), donors, cells_dev, block)
    fringe = fringe.reshape(inst_dev, nvars, cells_dev)
    total = own + faced + temporal + fringe - source
    return adjoint - dtau[None, None, :] * total


def spectral_blocks(inst_count, inst_dev):
    offset = np.arange(INSTANCES)[:, None] - np.arange(INSTANCES)[None, :]
    angle = offset * (np.pi / INSTANCES)
    parity = np.where(offset % 2 == 0, 1.0, -1.0)
    denom = np.where(offset == 0, 1.0, np.sin(angle))
    smat = np.where(offset == 0, 0.0, 0.25 * parity * np.cos(angle) / denom).astype(np.float32)
    high = smat.astype(ml_dtypes.bfloat16)
    low = (smat - high.astype(np.float32)).astype(ml_dtypes.bfloat16)
    blocks = []
    for me in range(inst_count):
        for hop in range(inst_count):
            other = (me - hop) % inst_count
            rows = []
            for part in (high, low):
                cut = part[other * inst_dev : (other + 1) * inst_dev, me * inst_dev : (me + 1) * inst_dev]
                wide = np.kron(np.eye(VARS, dtype=np.float32), cut.T.astype(np.float32))
                rows.append(np.concatenate([wide, wide], axis=1))
            blocks.append(np.concatenate(rows, axis=0))
    side = 2 * VARS * inst_dev
    stacked = np.stack(blocks).reshape(inst_count, inst_count, side, side)
    return jnp.asarray(stacked.astype(ml_dtypes.bfloat16))


def split_parts(value):
    high = value.astype(jnp.bfloat16)
    low = (value - high.astype(jnp.float32)).astype(jnp.bfloat16)
    return high, low


def step_kernel(
    ninst,
    npeer,
    adj_hbm,
    fsrc_hbm,
    fwt_hbm,
    cnt_hbm,
    nbr_hbm,
    fdst_hbm,
    face_hbm,
    diag_hbm,
    src_hbm,
    spec_hbm,
    dtau_hbm,
    out_ref,
    adj,
    fsrc,
    fwt,
    cnt,
    nbr,
    fdst,
    facej,
    diag,
    source,
    spec,
    dtau,
    parts,
    far,
    far_parts,
    near,
    faced,
    total,
    slots,
    coefs,
    packs,
    landed,
    values,
    place,
    load_sem,
    far_send,
    far_recv,
    fr_send,
    fr_recv,
):
    rows, cells = adj.shape
    idev = rows // VARS
    tiles = cells // TILE
    half = rows // 2
    pairs = npeer // 2
    cap = TILE // 2
    strip = tiles * FACES
    steps = pairs // 2
    my_inst = lax.axis_index("inst")
    my_cell = lax.axis_index("cell")

    ends = [
        (adj_hbm, adj),
        (fsrc_hbm, fsrc),
        (fwt_hbm, fwt),
        (cnt_hbm, cnt),
        (nbr_hbm, nbr),
        (fdst_hbm, fdst),
        (face_hbm, facej),
        (diag_hbm, diag),
        (src_hbm, source),
        (spec_hbm.at[my_inst], spec),
        (dtau_hbm, dtau),
    ]
    loads = [pltpu.make_async_copy(one, two, load_sem.at[at]) for at, (one, two) in enumerate(ends)]
    for load in loads[:4]:
        load.start()
    barrier = pltpu.get_barrier_semaphore()
    for hop in range(1, ninst):
        pl.semaphore_signal(
            barrier, inc=1, device_id=(lax.rem(my_inst + hop, ninst), my_cell), device_id_type=MESH
        )
    for hop in range(1, npeer):
        pl.semaphore_signal(
            barrier, inc=1, device_id=(my_inst, lax.rem(my_cell + hop, npeer)), device_id_type=MESH
        )
    for load in loads[4:]:
        load.start()

    lane = lax.broadcasted_iota(jnp.int32, (npeer, cap), 1)
    diagonal = lax.broadcasted_iota(jnp.int32, (npeer, npeer), 0) == lax.broadcasted_iota(
        jnp.int32, (npeer, npeer), 1
    )
    wide_low = lax.broadcasted_iota(jnp.int32, (half, TILE), 1) < cap
    window = lax.broadcasted_iota(jnp.int32, (256, 256), 0).astype(jnp.float32).astype(jnp.bfloat16)
    one, zero = jnp.bfloat16(1.0), jnp.bfloat16(0.0)

    def window_hits(ids, at):
        return jnp.where(window == (ids - 256 * at).astype(jnp.float32).astype(jnp.bfloat16), one, zero)

    for load in loads[1:4]:
        load.wait()
    slots[...] = jnp.concatenate([fsrc[0:pairs, :], fsrc[pairs:npeer, :]], axis=1)
    live_count = jnp.sum(
        jnp.where(diagonal, jnp.broadcast_to(cnt[...], (npeer, npeer)).astype(jnp.float32), 0.0), axis=1, keepdims=True
    )
    coef = jnp.where(lane.astype(jnp.float32) < live_count, fwt[...], 0.0)
    coefs[...] = jnp.concatenate([coef[0:pairs, :], coef[pairs:npeer, :]], axis=1)
    loads[0].wait()
    high, low = split_parts(adj[...])
    parts[0:rows, :] = high
    parts[rows:, :] = low

    def fringe_copy(peer, hop):
        return pltpu.make_async_remote_copy(
            src_ref=packs.at[peer],
            dst_ref=landed.at[my_cell],
            send_sem=fr_send.at[hop],
            recv_sem=fr_recv.at[hop],
            device_id=(my_inst, peer),
            device_id_type=MESH,
        )

    def pick_step(step):
        first = 2 * lax.rem(my_cell // 2 + step, steps)
        ids = jnp.concatenate([slots[pl.ds(first, 1), :], slots[pl.ds(first + 1, 1), :]], axis=1)
        both = jnp.zeros((2 * rows, 256), jnp.float32)
        for at in range(cells // 256):
            both = both + jnp.dot(
                parts[:, at * 256 : (at + 1) * 256],
                window_hits(ids, at),
                preferred_element_type=jnp.float32,
            )
        picked = both[0:rows, :] + both[rows:, :]
        for sub in range(2):
            pair = first + sub
            block = picked[:, sub * TILE : (sub + 1) * TILE] * coefs[pl.ds(pair, 1), :]
            upper, lower = block[0:half, :], block[half:, :]
            packs[pair] = jnp.where(wide_low, upper, pltpu.roll(lower, cap, 1))
            packs[pair + pairs] = jnp.where(wide_low, pltpu.roll(upper, cap, 1), lower)

    def send_step(step):
        first = 2 * lax.rem(my_cell // 2 + step, steps)
        for peer in (first + pairs, first + pairs + 1, first, first + 1):
            hop = lax.rem(peer - my_cell + npeer, npeer)

            @pl.when(hop != 0)
            def _():
                fringe_copy(peer, hop).start()

    early = 1
    for step in range(early):
        pick_step(step)
    pl.semaphore_wait(barrier, ninst + npeer - 2)
    far_copies = []
    for hop in range(1, ninst):
        copy = pltpu.make_async_remote_copy(
            src_ref=adj_hbm,
            dst_ref=far.at[hop - 1],
            send_sem=far_send.at[hop - 1],
            recv_sem=far_recv.at[hop - 1],
            device_id=(lax.rem(my_inst + hop, ninst), my_cell),
            device_id_type=MESH,
        )
        copy.start()
        far_copies.append(copy)
    for step in range(early):
        send_step(step)
    for step in range(early, steps):
        pick_step(step)
        send_step(step)
    landed[my_cell] = packs[my_cell]

    loads[4].wait()
    for tile in range(tiles):
        for face in range(FACES):
            other = jnp.broadcast_to(nbr[face : face + 1, tile : tile + 1], (idev, TILE))
            picks = [other == cand for cand in range(1, tiles)]
            for var in range(VARS):
                span = slice(var * idev, (var + 1) * idev)
                value = adj[span, 0:TILE]
                for cand in range(1, tiles):
                    value = jnp.where(picks[cand - 1], adj[span, cand * TILE : (cand + 1) * TILE], value)
                at = var * idev * strip + tile * FACES + face
                near[pl.ds(at, idev, stride=strip), :] = value

    loads[6].wait()

    def one_instance(inst, carry):
        sums = [jnp.zeros((strip, TILE), jnp.float32) for _ in range(VARS)]
        for var in range(VARS):
            start = pl.multiple_of((var * idev + inst) * strip, strip)
            beside = near[pl.ds(start, strip), :]
            for eqn in range(VARS):
                sums[eqn] = sums[eqn] + facej[inst, var, eqn].astype(jnp.float32) * beside
        for eqn in range(VARS):
            start = pl.multiple_of((eqn * idev + inst) * strip, strip)
            faced[pl.ds(start, strip), :] = sums[eqn]
        return carry

    lax.fori_loop(0, idev, one_instance, 0)

    for load in loads[7:10]:
        load.wait()
    both = jnp.dot(spec[0], parts[...], preferred_element_type=jnp.float32)
    total[...] = both[0:rows, :] + both[rows:, :]
    for tile in range(tiles):
        cols = slice(tile * TILE, (tile + 1) * TILE)
        mine = [adj[var * idev : (var + 1) * idev, cols] for var in range(VARS)]
        for eqn in range(VARS):
            span = slice(eqn * idev, (eqn + 1) * idev)
            value = total[span, cols] - source[span, cols]
            for var in range(VARS):
                value = value + diag[var, eqn, :, cols].astype(jnp.float32) * mine[var]
            for face in range(FACES):
                at = eqn * idev * strip + tile * FACES + face
                value = value + faced[pl.ds(at, idev, stride=strip), :]
            total[span, cols] = value

    loads[5].wait()
    loads[10].wait()
    for group in range(steps):
        pair = 2 * group
        ids = jnp.concatenate(
            [fdst[pair], fdst[pair + pairs], fdst[pair + 1], fdst[pair + 1 + pairs]], axis=1
        )
        for at in range(cells // 256):
            place[group, at * 256 : (at + 1) * 256, :] = window_hits(ids, at)

    def take_step(step):
        group = lax.rem(my_cell // 2 - step + steps, steps)
        first = 2 * group
        for origin in (first, first + 1, first + pairs, first + pairs + 1):
            hop = lax.rem(my_cell - origin + npeer, npeer)

            @pl.when(hop != 0)
            def _():
                fringe_copy(lax.rem(my_cell + hop, npeer), hop).wait_recv()

        for sub in range(2):
            here, there = landed[first + sub], landed[first + sub + pairs]
            cols = slice(sub * TILE, (sub + 1) * TILE)
            high, low = split_parts(jnp.where(wide_low, here, pltpu.roll(there, cap, 1)))
            values[0:half, cols] = high
            values[rows : rows + half, cols] = low
            high, low = split_parts(jnp.where(wide_low, pltpu.roll(here, cap, 1), there))
            values[half:rows, cols] = high
            values[rows + half :, cols] = low
        for at in range(cells // 256):
            both = lax.dot_general(
                values[...],
                place[group, at * 256 : (at + 1) * 256, :],
                (((1,), (1,)), ((), ())),
                preferred_element_type=jnp.float32,
            )
            fringe = both[0:rows, :] + both[rows:, :]
            for sub in range(2):
                tile = at * 2 + sub
                cols = slice(tile * TILE, (tile + 1) * TILE)
                whole = total[:, cols] + fringe[:, sub * TILE : (sub + 1) * TILE]
                if step < steps - 1:
                    total[:, cols] = whole
                else:
                    out_ref[:, cols] = adj[:, cols] - dtau[tile : tile + 1, :] * whole

    for step in range(steps // 2):
        take_step(step)
    for hop in range(1, ninst):
        far_copies[hop - 1].wait_recv()
        high, low = split_parts(far[hop - 1])
        far_parts[0:rows, :] = high
        far_parts[rows:, :] = low
        both = jnp.dot(spec[hop], far_parts[...], preferred_element_type=jnp.float32)
        total[...] += both[0:rows, :] + both[rows:, :]
    for step in range(steps // 2, steps):
        take_step(step)

    for copy in far_copies:
        copy.wait_send()
    for hop in range(1, npeer):
        fringe_copy(lax.rem(my_cell + hop, npeer), hop).wait_send()


def store_kernel(held, out_hbm, sems):
    span = held.shape[0] // VARS
    copies = []
    for var in range(VARS):
        rows = pl.ds(var * span, span)
        copies.append(pltpu.make_async_copy(held.at[rows], out_hbm.at[rows], sems.at[var]))
    for copy in copies:
        copy.start()
    for copy in copies:
        copy.wait()


def fused_step(
    ninst,
    npeer,
    adjoint,
    source,
    jac_diag,
    jac_face,
    tile_nbr,
    dtau,
    fringe_src,
    fringe_wt,
    fringe_count,
    fringe_dst,
):
    idev, nvars, cells = adjoint.shape
    tiles = cells // TILE
    rows = idev * nvars
    pairs = npeer // 2
    strip = tiles * FACES
    adj = jnp.transpose(adjoint, (1, 0, 2)).reshape(rows, cells)
    src = jnp.transpose(source, (1, 0, 2)).reshape(rows, cells)
    diag = jnp.transpose(jac_diag, (1, 2, 0, 3))
    face = jac_face.reshape(idev, FACES, nvars, nvars, tiles, TILE)
    face = jnp.transpose(face, (0, 2, 3, 4, 1, 5)).reshape(idev, nvars, nvars, strip, TILE)
    spectral = spectral_blocks(ninst, idev)
    operands = [
        adj,
        fringe_src[0],
        fringe_wt[0],
        fringe_count,
        tile_nbr.T,
        fringe_dst,
        face,
        diag,
        src,
        spectral,
        dtau.reshape(tiles, TILE),
    ]
    held = [pltpu.VMEM(one.shape, one.dtype) for one in operands]
    held[9] = pltpu.VMEM(spectral.shape[1:], spectral.dtype)
    out = pl.pallas_call(
        functools.partial(step_kernel, ninst, npeer),
        out_shape=pltpu.VMEM((rows, cells), jnp.float32),
        in_specs=[pl.BlockSpec(memory_space=pltpu.HBM)] * len(operands),
        out_specs=pl.BlockSpec(memory_space=pltpu.VMEM),
        scratch_shapes=held
        + [
            pltpu.VMEM((2 * rows, cells), jnp.bfloat16),
            pltpu.VMEM((ninst - 1, rows, cells), jnp.float32),
            pltpu.VMEM((2 * rows, cells), jnp.bfloat16),
            pltpu.VMEM((rows * strip, TILE), jnp.float32),
            pltpu.VMEM((rows * strip, TILE), jnp.float32),
            pltpu.VMEM((rows, cells), jnp.float32),
            pltpu.VMEM((pairs, TILE), jnp.int32),
            pltpu.VMEM((pairs, TILE), jnp.float32),
            pltpu.VMEM((npeer, rows // 2, TILE), jnp.float32),
            pltpu.VMEM((npeer, rows // 2, TILE), jnp.float32),
            pltpu.VMEM((2 * rows, 256), jnp.bfloat16),
            pltpu.VMEM((pairs // 2, cells, 256), jnp.bfloat16),
            pltpu.SemaphoreType.DMA((len(operands),)),
            pltpu.SemaphoreType.DMA((ninst - 1,)),
            pltpu.SemaphoreType.DMA((ninst - 1,)),
            pltpu.SemaphoreType.DMA((npeer,)),
            pltpu.SemaphoreType.DMA((npeer,)),
        ],
        compiler_params=pltpu.CompilerParams(
            collective_id=0, has_side_effects=True, vmem_limit_bytes=56 * 1024 * 1024
        ),
    )(*operands)
    out = pl.pallas_call(
        store_kernel,
        out_shape=jax.ShapeDtypeStruct((rows, cells), jnp.float32),
        in_specs=[pl.BlockSpec(memory_space=pltpu.VMEM)],
        out_specs=pl.BlockSpec(memory_space=pltpu.HBM),
        scratch_shapes=[pltpu.SemaphoreType.DMA((nvars,))],
    )(out)
    return jnp.transpose(out.reshape(nvars, idev, cells), (1, 0, 2))


def solution(mesh):
    placed = (
        P("inst", None, "cell"),
        P("inst", None, "cell"),
        P("inst", None, None, "cell"),
        P("inst", None, None, None, "cell"),
        P("cell", None),
        P("cell"),
        P("cell", None, None),
        P("cell", None, None),
        P("cell", None),
        P(None, "cell", None),
    )
    ninst, npeer = mesh.shape["inst"], mesh.shape["cell"]

    def body(adjoint, *rest):
        idev, _, cells = adjoint.shape
        slot_cap = rest[5].shape[2]
        fits = idev % 8 == 0 and ninst > 1 and npeer % 4 == 0
        if fits and cells % 256 == 0 and slot_cap * 2 == TILE:
            return fused_step(ninst, npeer, adjoint, *rest)
        return on_device(adjoint, *rest)

    return jax.shard_map(
        body, mesh=mesh, in_specs=placed, out_specs=P("inst", None, "cell"), check_vma=False
    )
```

```python
import functools
import math

import jax
import jax.numpy as jnp
import ml_dtypes
import numpy as np
from jax import lax
from jax.experimental import pallas as pl
from jax.experimental.pallas import tpu as pltpu
from jax.sharding import PartitionSpec as P

INSTANCES = 16
FACES = 4
TILE = 128
VARS = 6
MESH = pl.DeviceIdType.MESH


def spectral_matrix(count):
    rows = jnp.arange(count, dtype=jnp.int32)[:, None]
    cols = jnp.arange(count, dtype=jnp.int32)[None, :]
    offset = rows - cols
    angle = offset.astype(jnp.float32) * (jnp.pi / count)
    parity = jnp.where(offset % 2 == 0, 1.0, -1.0).astype(jnp.float32)
    denom = jnp.where(offset == 0, 1.0, jnp.sin(angle))
    value = 0.25 * parity * jnp.cos(angle) / denom
    return jnp.where(offset == 0, 0.0, value)


def pick_rows(flat, sources, weights, block):
    cells_dev = flat.shape[1]
    nblocks = sources.shape[0] // block
    cell_ids = jnp.arange(cells_dev, dtype=jnp.int32)[:, None]

    def one_block(pair):
        index_block, weight_block = pair
        select = jnp.where(cell_ids == index_block[None, :], weight_block[None, :], 0.0)
        return jnp.dot(
            flat, select, precision=lax.Precision.HIGHEST, preferred_element_type=jnp.float32
        )

    result = lax.map(one_block, (sources.reshape(nblocks, block), weights.reshape(nblocks, block)))
    return jnp.transpose(result, (1, 0, 2)).reshape(flat.shape[0], -1)


def place_rows(values, targets, cells_dev, block):
    nblocks = targets.shape[0] // block
    cell_ids = jnp.arange(cells_dev, dtype=jnp.int32)[None, :]

    def add_block(step, total):
        start = step * block
        target_block = lax.dynamic_slice_in_dim(targets, start, block, 0)
        value_block = lax.dynamic_slice_in_dim(values, start, block, 1)
        select = jnp.where(target_block[:, None] == cell_ids, 1.0, 0.0).astype(jnp.float32)
        return total + jnp.dot(
            value_block, select, precision=lax.Precision.HIGHEST, preferred_element_type=jnp.float32
        )

    empty = jnp.zeros((values.shape[0], cells_dev), jnp.float32)
    return lax.fori_loop(0, nblocks, add_block, empty)


def on_device(
    adjoint,
    source,
    jac_diag,
    jac_face,
    tile_nbr,
    dtau,
    fringe_src,
    fringe_wt,
    fringe_count,
    fringe_dst,
):
    inst_dev, nvars, cells_dev = adjoint.shape
    tiles_dev = cells_dev // TILE
    peer_count, slot_cap = (fringe_wt.shape[1], fringe_wt.shape[2])
    total_slots = peer_count * slot_cap
    block = math.gcd(total_slots, 512)
    smat = spectral_matrix(INSTANCES)
    flat = adjoint.reshape(inst_dev * nvars, cells_dev)
    live = jnp.arange(slot_cap, dtype=jnp.int32)[None, :] < fringe_count[0][:, None]
    coef = jnp.where(live, fringe_wt[0], 0.0).reshape(-1)
    picked = pick_rows(flat, fringe_src[0].reshape(-1), coef, block)
    outgoing = picked.reshape(inst_dev, nvars, peer_count, slot_cap)
    arrived = lax.all_to_all(outgoing, "cell", split_axis=2, concat_axis=2, tiled=True)
    spread = lax.all_to_all(adjoint, "inst", split_axis=2, concat_axis=0, tiled=True)
    mixed = jnp.einsum("ji,jac->iac", smat, spread, precision=lax.Precision.HIGHEST)
    temporal = lax.all_to_all(mixed, "inst", split_axis=0, concat_axis=2, tiled=True)
    own = jnp.sum(jac_diag.astype(jnp.float32) * adjoint[:, :, None, :], axis=1)
    tiles = adjoint.reshape(inst_dev, nvars, tiles_dev, TILE)
    tile_ids = jnp.arange(tiles_dev, dtype=jnp.int32)[None, :]
    faced = jnp.zeros_like(adjoint)
    for face in range(FACES):
        select = jnp.where(tile_nbr[:, face][:, None] == tile_ids, 1.0, 0.0).astype(jnp.float32)
        near = jnp.einsum("tu,iaup->iatp", select, tiles, precision=lax.Precision.HIGHEST)
        near = near.reshape(inst_dev, nvars, cells_dev)
        faced = faced + jnp.sum(jac_face[:, face].astype(jnp.float32) * near[:, :, None, :], axis=1)
    donors = fringe_dst[:, 0, :].reshape(-1)
    fringe = place_rows(arrived.reshape(inst_dev * nvars, -1), donors, cells_dev, block)
    fringe = fringe.reshape(inst_dev, nvars, cells_dev)
    total = own + faced + temporal + fringe - source
    return adjoint - dtau[None, None, :] * total


def spectral_blocks(inst_count, inst_dev):
    offset = np.arange(INSTANCES)[:, None] - np.arange(INSTANCES)[None, :]
    angle = offset * (np.pi / INSTANCES)
    parity = np.where(offset % 2 == 0, 1.0, -1.0)
    denom = np.where(offset == 0, 1.0, np.sin(angle))
    smat = np.where(offset == 0, 0.0, 0.25 * parity * np.cos(angle) / denom).astype(np.float32)
    high = smat.astype(ml_dtypes.bfloat16)
    low = (smat - high.astype(np.float32)).astype(ml_dtypes.bfloat16)
    blocks = []
    for me in range(inst_count):
        for hop in range(inst_count):
            other = (me - hop) % inst_count
            rows = []
            for part in (high, low):
                cut = part[other * inst_dev : (other + 1) * inst_dev, me * inst_dev : (me + 1) * inst_dev]
                wide = np.kron(np.eye(VARS, dtype=np.float32), cut.T.astype(np.float32))
                rows.append(np.concatenate([wide, wide], axis=1))
            blocks.append(np.concatenate(rows, axis=0))
    side = 2 * VARS * inst_dev
    stacked = np.stack(blocks).reshape(inst_count, inst_count, side, side)
    return jnp.asarray(stacked.astype(ml_dtypes.bfloat16))


def split_parts(value):
    high = value.astype(jnp.bfloat16)
    low = (value - high.astype(jnp.float32)).astype(jnp.bfloat16)
    return high, low


def step_kernel(
    ninst,
    npeer,
    adj_hbm,
    fsrc_hbm,
    fwt_hbm,
    cnt_hbm,
    nbr_hbm,
    fdst_hbm,
    face_hbm,
    diag_hbm,
    src_hbm,
    spec_hbm,
    dtau_hbm,
    out_ref,
    adj,
    fsrc,
    fwt,
    cnt,
    nbr,
    fdst,
    facej,
    diag,
    source,
    spec,
    dtau,
    parts,
    far,
    far_parts,
    near,
    faced,
    total,
    slots,
    coefs,
    packs,
    landed,
    values,
    place,
    load_sem,
    far_send,
    far_recv,
    fr_send,
    fr_recv,
):
    rows, cells = adj.shape
    idev = rows // VARS
    tiles = cells // TILE
    half = rows // 2
    pairs = npeer // 2
    cap = TILE // 2
    strip = tiles * FACES
    steps = pairs // 2
    my_inst = lax.axis_index("inst")
    my_cell = lax.axis_index("cell")

    ends = [
        (adj_hbm, adj),
        (fsrc_hbm, fsrc),
        (fwt_hbm, fwt),
        (cnt_hbm, cnt),
        (nbr_hbm, nbr),
        (fdst_hbm, fdst),
        (face_hbm, facej),
        (diag_hbm, diag),
        (src_hbm, source),
        (spec_hbm.at[my_inst], spec),
        (dtau_hbm, dtau),
    ]
    loads = [pltpu.make_async_copy(one, two, load_sem.at[at]) for at, (one, two) in enumerate(ends)]
    for load in loads[:4]:
        load.start()
    barrier = pltpu.get_barrier_semaphore()
    for hop in range(1, ninst):
        pl.semaphore_signal(
            barrier, inc=1, device_id=(lax.rem(my_inst + hop, ninst), my_cell), device_id_type=MESH
        )
    for hop in range(1, npeer):
        pl.semaphore_signal(
            barrier, inc=1, device_id=(my_inst, lax.rem(my_cell + hop, npeer)), device_id_type=MESH
        )
    for load in loads[4:]:
        load.start()

    lane = lax.broadcasted_iota(jnp.int32, (npeer, cap), 1)
    diagonal = lax.broadcasted_iota(jnp.int32, (npeer, npeer), 0) == lax.broadcasted_iota(
        jnp.int32, (npeer, npeer), 1
    )
    wide_low = lax.broadcasted_iota(jnp.int32, (half, TILE), 1) < cap
    window = lax.broadcasted_iota(jnp.int32, (256, 256), 0).astype(jnp.float32).astype(jnp.bfloat16)
    one, zero = jnp.bfloat16(1.0), jnp.bfloat16(0.0)

    def window_hits(ids, at):
        return jnp.where(window == (ids - 256 * at).astype(jnp.float32).astype(jnp.bfloat16), one, zero)

    for load in loads[1:4]:
        load.wait()
    slots[...] = jnp.concatenate([fsrc[0:pairs, :], fsrc[pairs:npeer, :]], axis=1)
    live_count = jnp.sum(
        jnp.where(diagonal, jnp.broadcast_to(cnt[...], (npeer, npeer)).astype(jnp.float32), 0.0), axis=1, keepdims=True
    )
    coef = jnp.where(lane.astype(jnp.float32) < live_count, fwt[...], 0.0)
    coefs[...] = jnp.concatenate([coef[0:pairs, :], coef[pairs:npeer, :]], axis=1)
    loads[0].wait()
    high, low = split_parts(adj[...])
    parts[0:rows, :] = high
    parts[rows:, :] = low

    def fringe_copy(peer, hop):
        return pltpu.make_async_remote_copy(
            src_ref=packs.at[peer],
            dst_ref=landed.at[my_cell],
            send_sem=fr_send.at[hop],
            recv_sem=fr_recv.at[hop],
            device_id=(my_inst, peer),
            device_id_type=MESH,
        )

    def pick_step(step):
        first = 2 * lax.rem(my_cell // 2 + step, steps)
        ids = jnp.concatenate([slots[pl.ds(first, 1), :], slots[pl.ds(first + 1, 1), :]], axis=1)
        both = jnp.zeros((2 * rows, 256), jnp.float32)
        for at in range(cells // 256):
            both = both + jnp.dot(
                parts[:, at * 256 : (at + 1) * 256],
                window_hits(ids, at),
                preferred_element_type=jnp.float32,
            )
        picked = both[0:rows, :] + both[rows:, :]
        for sub in range(2):
            pair = first + sub
            block = picked[:, sub * TILE : (sub + 1) * TILE] * coefs[pl.ds(pair, 1), :]
            upper, lower = block[0:half, :], block[half:, :]
            packs[pair] = jnp.where(wide_low, upper, pltpu.roll(lower, cap, 1))
            packs[pair + pairs] = jnp.where(wide_low, pltpu.roll(upper, cap, 1), lower)

    def send_step(step):
        first = 2 * lax.rem(my_cell // 2 + step, steps)
        for peer in (first + pairs, first + pairs + 1, first, first + 1):
            hop = lax.rem(peer - my_cell + npeer, npeer)

            @pl.when(hop != 0)
            def _():
                fringe_copy(peer, hop).start()

    early = 1
    for step in range(early):
        pick_step(step)
    pl.semaphore_wait(barrier, ninst + npeer - 2)
    far_copies = []
    for hop in range(1, ninst):
        copy = pltpu.make_async_remote_copy(
            src_ref=adj_hbm,
            dst_ref=far.at[hop - 1],
            send_sem=far_send.at[hop - 1],
            recv_sem=far_recv.at[hop - 1],
            device_id=(lax.rem(my_inst + hop, ninst), my_cell),
            device_id_type=MESH,
        )
        copy.start()
        far_copies.append(copy)
    for step in range(early):
        send_step(step)
    for step in range(early, steps):
        pick_step(step)
        send_step(step)
    landed[my_cell] = packs[my_cell]

    loads[4].wait()
    for tile in range(tiles):
        for face in range(FACES):
            other = jnp.broadcast_to(nbr[face : face + 1, tile : tile + 1], (idev, TILE))
            picks = [other == cand for cand in range(1, tiles)]
            for var in range(VARS):
                span = slice(var * idev, (var + 1) * idev)
                value = adj[span, 0:TILE]
                for cand in range(1, tiles):
                    value = jnp.where(picks[cand - 1], adj[span, cand * TILE : (cand + 1) * TILE], value)
                at = var * idev * strip + tile * FACES + face
                near[pl.ds(at, idev, stride=strip), :] = value

    loads[6].wait()

    def one_instance(inst, carry):
        sums = [jnp.zeros((strip, TILE), jnp.float32) for _ in range(VARS)]
        for var in range(VARS):
            start = pl.multiple_of((var * idev + inst) * strip, strip)
            beside = near[pl.ds(start, strip), :]
            for eqn in range(VARS):
                sums[eqn] = sums[eqn] + facej[inst, var, eqn].astype(jnp.float32) * beside
        for eqn in range(VARS):
            start = pl.multiple_of((eqn * idev + inst) * strip, strip)
            faced[pl.ds(start, strip), :] = sums[eqn]
        return carry

    lax.fori_loop(0, idev, one_instance, 0)

    for load in loads[7:10]:
        load.wait()
    both = jnp.dot(spec[0], parts[...], preferred_element_type=jnp.float32)
    total[...] = both[0:rows, :] + both[rows:, :]
    for tile in range(tiles):
        cols = slice(tile * TILE, (tile + 1) * TILE)
        mine = [adj[var * idev : (var + 1) * idev, cols] for var in range(VARS)]
        for eqn in range(VARS):
            span = slice(eqn * idev, (eqn + 1) * idev)
            value = total[span, cols] - source[span, cols]
            for var in range(VARS):
                value = value + diag[var, eqn, :, cols].astype(jnp.float32) * mine[var]
            for face in range(FACES):
                at = eqn * idev * strip + tile * FACES + face
                value = value + faced[pl.ds(at, idev, stride=strip), :]
            total[span, cols] = value

    loads[5].wait()
    loads[10].wait()
    for group in range(steps):
        pair = 2 * group
        ids = jnp.concatenate(
            [fdst[pair], fdst[pair + pairs], fdst[pair + 1], fdst[pair + 1 + pairs]], axis=1
        )
        for at in range(cells // 256):
            place[group, at * 256 : (at + 1) * 256, :] = window_hits(ids, at)

    def take_step(step):
        group = lax.rem(my_cell // 2 - step + steps, steps)
        first = 2 * group
        for origin in (first, first + 1, first + pairs, first + pairs + 1):
            hop = lax.rem(my_cell - origin + npeer, npeer)

            @pl.when(hop != 0)
            def _():
                fringe_copy(lax.rem(my_cell + hop, npeer), hop).wait_recv()

        for sub in range(2):
            here, there = landed[first + sub], landed[first + sub + pairs]
            cols = slice(sub * TILE, (sub + 1) * TILE)
            high, low = split_parts(jnp.where(wide_low, here, pltpu.roll(there, cap, 1)))
            values[0:half, cols] = high
            values[rows : rows + half, cols] = low
            high, low = split_parts(jnp.where(wide_low, pltpu.roll(here, cap, 1), there))
            values[half:rows, cols] = high
            values[rows + half :, cols] = low
        for at in range(cells // 256):
            both = lax.dot_general(
                values[...],
                place[group, at * 256 : (at + 1) * 256, :],
                (((1,), (1,)), ((), ())),
                preferred_element_type=jnp.float32,
            )
            fringe = both[0:rows, :] + both[rows:, :]
            for sub in range(2):
                tile = at * 2 + sub
                cols = slice(tile * TILE, (tile + 1) * TILE)
                whole = total[:, cols] + fringe[:, sub * TILE : (sub + 1) * TILE]
                if step < steps - 1:
                    total[:, cols] = whole
                else:
                    out_ref[:, cols] = adj[:, cols] - dtau[tile : tile + 1, :] * whole

    for step in range(steps // 2):
        take_step(step)
    for hop in range(1, ninst):
        far_copies[hop - 1].wait_recv()
        high, low = split_parts(far[hop - 1])
        far_parts[0:rows, :] = high
        far_parts[rows:, :] = low
        both = jnp.dot(spec[hop], far_parts[...], preferred_element_type=jnp.float32)
        total[...] += both[0:rows, :] + both[rows:, :]
    for step in range(steps // 2, steps):
        take_step(step)

    for copy in far_copies:
        copy.wait_send()
    for hop in range(1, npeer):
        fringe_copy(lax.rem(my_cell + hop, npeer), hop).wait_send()


def store_kernel(held, out_hbm, sems):
    span = held.shape[0] // VARS
    copies = []
    for var in range(VARS):
        rows = pl.ds(var * span, span)
        copies.append(pltpu.make_async_copy(held.at[rows], out_hbm.at[rows], sems.at[var]))
    for copy in copies:
        copy.start()
    for copy in copies:
        copy.wait()


def fused_step(
    ninst,
    npeer,
    adjoint,
    source,
    jac_diag,
    jac_face,
    tile_nbr,
    dtau,
    fringe_src,
    fringe_wt,
    fringe_count,
    fringe_dst,
):
    idev, nvars, cells = adjoint.shape
    tiles = cells // TILE
    rows = idev * nvars
    pairs = npeer // 2
    strip = tiles * FACES
    adj = jnp.transpose(adjoint, (1, 0, 2)).reshape(rows, cells)
    src = jnp.transpose(source, (1, 0, 2)).reshape(rows, cells)
    diag = jnp.transpose(jac_diag, (1, 2, 0, 3))
    face = jac_face.reshape(idev, FACES, nvars, nvars, tiles, TILE)
    face = jnp.transpose(face, (0, 2, 3, 4, 1, 5)).reshape(idev, nvars, nvars, strip, TILE)
    spectral = spectral_blocks(ninst, idev)
    operands = [
        adj,
        fringe_src[0],
        fringe_wt[0],
        fringe_count,
        tile_nbr.T,
        fringe_dst,
        face,
        diag,
        src,
        spectral,
        dtau.reshape(tiles, TILE),
    ]
    held = [pltpu.VMEM(one.shape, one.dtype) for one in operands]
    held[9] = pltpu.VMEM(spectral.shape[1:], spectral.dtype)
    out = pl.pallas_call(
        functools.partial(step_kernel, ninst, npeer),
        out_shape=pltpu.VMEM((rows, cells), jnp.float32),
        in_specs=[pl.BlockSpec(memory_space=pltpu.HBM)] * len(operands),
        out_specs=pl.BlockSpec(memory_space=pltpu.VMEM),
        scratch_shapes=held
        + [
            pltpu.VMEM((2 * rows, cells), jnp.bfloat16),
            pltpu.VMEM((ninst - 1, rows, cells), jnp.float32),
            pltpu.VMEM((2 * rows, cells), jnp.bfloat16),
            pltpu.VMEM((rows * strip, TILE), jnp.float32),
            pltpu.VMEM((rows * strip, TILE), jnp.float32),
            pltpu.VMEM((rows, cells), jnp.float32),
            pltpu.VMEM((pairs, TILE), jnp.int32),
            pltpu.VMEM((pairs, TILE), jnp.float32),
            pltpu.VMEM((npeer, rows // 2, TILE), jnp.float32),
            pltpu.VMEM((npeer, rows // 2, TILE), jnp.float32),
            pltpu.VMEM((2 * rows, 256), jnp.bfloat16),
            pltpu.VMEM((pairs // 2, cells, 256), jnp.bfloat16),
            pltpu.SemaphoreType.DMA((len(operands),)),
            pltpu.SemaphoreType.DMA((ninst - 1,)),
            pltpu.SemaphoreType.DMA((ninst - 1,)),
            pltpu.SemaphoreType.DMA((npeer,)),
            pltpu.SemaphoreType.DMA((npeer,)),
        ],
        compiler_params=pltpu.CompilerParams(
            collective_id=0, has_side_effects=True, vmem_limit_bytes=56 * 1024 * 1024
        ),
    )(*operands)
    out = pl.pallas_call(
        store_kernel,
        out_shape=jax.ShapeDtypeStruct((rows, cells), jnp.float32),
        in_specs=[pl.BlockSpec(memory_space=pltpu.VMEM)],
        out_specs=pl.BlockSpec(memory_space=pltpu.HBM),
        scratch_shapes=[pltpu.SemaphoreType.DMA((nvars,))],
        compiler_params=pltpu.CompilerParams(vmem_limit_bytes=1024 * 1024),
    )(out)
    return jnp.transpose(out.reshape(nvars, idev, cells), (1, 0, 2))


def solution(mesh):
    placed = (
        P("inst", None, "cell"),
        P("inst", None, "cell"),
        P("inst", None, None, "cell"),
        P("inst", None, None, None, "cell"),
        P("cell", None),
        P("cell"),
        P("cell", None, None),
        P("cell", None, None),
        P("cell", None),
        P(None, "cell", None),
    )
    ninst, npeer = mesh.shape["inst"], mesh.shape["cell"]

    def body(adjoint, *rest):
        idev, _, cells = adjoint.shape
        slot_cap = rest[5].shape[2]
        fits = idev % 8 == 0 and ninst > 1 and npeer % 4 == 0
        if fits and cells % 256 == 0 and slot_cap * 2 == TILE:
            return fused_step(ninst, npeer, adjoint, *rest)
        return on_device(adjoint, *rest)

    return jax.shard_map(
        body, mesh=mesh, in_specs=placed, out_specs=P("inst", None, "cell"), check_vma=False
    )
```
